32 devices in a mesh: layers: 2 (over y), rows: 4 (over z), cols: 4 (over x, core).
Axes of the slice: x: 2, y: 2, z: 4, core: 2. Of those that a mesh axis runs over, the one named last changes fastest.
Arguments:
- weight: bfloat16 [2048, 16384], P(('layers', 'rows'), 'cols'), parts along dimension 0, may hold values from -6 to 6
- update: bfloat16 [2048, 16384], P(('layers', 'rows'), 'cols'), parts along dimension 0, may hold values from -4 to 4
- keep_codes: int32 [2048, 2048], P(('layers', 'rows'), 'cols'), parts along dimension 0, may hold values from 0 to 35
- chol_factor: bfloat16 [32768, 16384], P(('layers', 'cols'), 'rows'), parts along dimension 0, as said below
- sketch: bfloat16 [16384, 256], P('rows'), may hold values from -6 to 6
Outputs:
- adapter_a: bfloat16 [2048, 256], P(('layers', 'rows')), parts along dimension 0
- adapter_b: bfloat16 [512, 16384], P(('layers', 'rows'), 'cols'), parts along dimension 0
The draws below stay inside these ranges and needn't reach their ends.
There are 2 independent parts, one for each index of `layers`. The reference program is written for one: setup_inputs(seed, part) draws one part's arguments, and reference() takes and returns one part's arrays. A program takes and returns all parts, laid end to end along the dimension named above; an argument that names none is the same for every part. Nothing has to cross between parts.
Inputs may be any that keep to these rules, and one draw needn't show every extreme that they name: `keep_codes`: each code is a pair of 2:4 patterns, the first in code % 6 and the second in code // 6. chol_factor is lower triangular with a positive diagonal.
All inputs are finite; a program needn't handle non-finite values.
Results may differ from the reference program's by a relative error of at most 0.006.
Values may be sent and summed in bfloat16 or wider, within the bound.
A program may use at most 128 MiB of HBM per device.

```python
import math
import jax
import jax.numpy as jnp
from jax import lax

D = 16384
R = 256
ROWS = 1024


def draw_chol_factor(key, part):
    entry_key = jax.random.fold_in(key, 11)
    scale_key = jax.random.fold_in(key, 23)
    row_index = jnp.arange(D)[:, None]
    col_index = jnp.arange(D)[None, :]
    entries = jax.random.normal(entry_key, (D, D), jnp.float32)
    row_scale = jnp.exp(jax.random.uniform(scale_key, (D, 1), jnp.float32, 0.0, math.log(10.0)))
    below = 0.6 * entries / jnp.sqrt(row_index.astype(jnp.float32) + 1.0)
    factor = jnp.where(col_index < row_index, below, jnp.where(col_index == row_index, 1.0, 0.0))
    return (row_scale * factor).astype(jnp.bfloat16)


def plant(drawn, rng, least, largest):
    dims = drawn.shape
    place = [jax.random.randint(jax.random.fold_in(rng, axis), (), 0, dims[axis]) for axis in range(len(dims))]
    drawn = drawn.at[tuple(place)].set(least)
    longest = dims.index(max(dims))
    place[longest] = (place[longest] + 1) % dims[longest]
    return drawn.at[tuple(place)].set(largest)


def block_scale(rng, shape, pieces, least, largest):
    factor_of = 1.0
    for axis_at, blocks in pieces:
        draws = jax.random.uniform(jax.random.fold_in(jax.random.fold_in(rng, 6), axis_at), (blocks,), jnp.float32, least / len(pieces), largest / len(pieces))
        factor_of = factor_of * jnp.repeat(jnp.exp(draws), shape[axis_at] // blocks).reshape((-1,) + (1,) * (len(shape) - 1 - axis_at))
    return factor_of


def centred(own_key, shape, spread, reach, split=(), dtype=jnp.bfloat16):
    drawn = spread * jax.random.normal(own_key, shape, jnp.float32)
    if split:
        drawn = drawn * block_scale(own_key, shape, split, -0.22, 0.18)
    return jnp.clip(drawn, -reach, reach).astype(dtype)


def setup_inputs(seed: int = 0, part: int = 0) -> dict:
    arg_keys = jax.random.split(jax.random.key(seed), 6)
    own_keys = jax.random.split(jax.random.fold_in(arg_keys[5], part), 6)
    return {
        "weight": centred(own_keys[0], (ROWS, D), 1.0, 6.0, ((0, 4), (1, 4))),
        "update": centred(own_keys[1], (ROWS, D), 0.5, 4.0, ((0, 4), (1, 4))),
        "keep_codes": plant(jax.random.randint(own_keys[2], (ROWS, D // 8), 0, 36), jax.random.fold_in(own_keys[2], 1), 0, 35).astype(jnp.int32),
        "chol_factor": draw_chol_factor(jax.random.fold_in(jax.random.fold_in(arg_keys[5], part), 71), part),
        "sketch": centred(arg_keys[4], (D, R), 1.0, 6.0, ((0, 4),)),
    }


def decode_keep(codes):
    first = codes % 6
    second = codes // 6
    columns = []
    for part_code in (first, second):
        columns.append(((part_code == 0) | (part_code == 1) | (part_code == 2)).astype(jnp.float32))
        columns.append(((part_code == 0) | (part_code == 3) | (part_code == 4)).astype(jnp.float32))
        columns.append(((part_code == 1) | (part_code == 3) | (part_code == 5)).astype(jnp.float32))
        columns.append(((part_code == 2) | (part_code == 4) | (part_code == 5)).astype(jnp.float32))
    stacked = jnp.stack(columns, axis=-1)
    return stacked.reshape(codes.shape[0], codes.shape[1] * 8)

def reference(weight, update, keep_codes, chol_factor, sketch):
    kept_mask = decode_keep(keep_codes)
    weight_f = weight.astype(jnp.float32)
    prune_error = (weight_f - kept_mask * (weight_f + update.astype(jnp.float32))).astype(jnp.bfloat16)
    whitened = jnp.dot(chol_factor.astype(jnp.float32), sketch.astype(jnp.float32), preferred_element_type=jnp.float32).astype(jnp.bfloat16)
    sample = jnp.dot(prune_error.astype(jnp.float32), whitened.astype(jnp.float32), preferred_element_type=jnp.float32)
    gram_matrix = jnp.dot(sample.T.astype(jnp.float32), sample.astype(jnp.float32), precision=lax.Precision.HIGHEST, preferred_element_type=jnp.float32)
    lower_factor = jnp.linalg.cholesky(gram_matrix)
    basis_cols = lax.linalg.triangular_solve(lower_factor, sample, left_side=False, lower=True, transpose_a=True)
    root_rows = math.sqrt(ROWS)
    adapter_a = (root_rows * basis_cols).astype(jnp.bfloat16)
    adapter_b = (jnp.dot(adapter_a.T.astype(jnp.float32), prune_error.astype(jnp.float32), preferred_element_type=jnp.float32) / root_rows).astype(jnp.bfloat16)
    return (adapter_a, adapter_b)
```

```python
import functools
import math

import jax
import jax.numpy as jnp
from jax import lax
from jax.experimental import pallas as pl
from jax.experimental.pallas import tpu as pltpu
from jax.sharding import PartitionSpec as P

MESH = pl.DeviceIdType.MESH
F32 = jnp.float32
BF16 = jnp.bfloat16
NCHUNK = 8
WORDS = 128

HI = lax.Precision.HIGHEST

def chol_steps(m_ref, w_ref, n, nseg):
    row = lax.broadcasted_iota(jnp.int32, (n, n), 0)
    col = lax.broadcasted_iota(jnp.int32, (n, n), 1)
    w_ref[...] = jnp.where(row == col, 1.0, 0.0).astype(jnp.float32)
    seg = n // nseg
    sub = lax.broadcasted_iota(jnp.int32, (8, 128), 0)
    for s in range(nseg):
        base = s * seg
        rows = n - base
        width = max(128, -(-rows // 128) * 128)
        wwidth = max(128, -(-(base + seg) // 128) * 128)
        rid = lax.broadcasted_iota(jnp.int32, (rows, 128), 0) + base

        def body(i, carry, base=base, rows=rows, width=width, wwidth=wwidth, rid=rid):
            r0 = pl.multiple_of(base + i * 8, 8)
            m = m_ref[base:n, :width]
            c = [jnp.broadcast_to(m[:, j:j + 1], (rows, 128)) for j in range(8)]
            b8 = m_ref[pl.ds(r0, 8), 0:128]
            p = [jnp.broadcast_to(b8[:, j:j + 1], (8, 128)) for j in range(8)]
            rm = m_ref[pl.ds(r0, 8), :width]
            rw = w_ref[pl.ds(r0, 8), :wwidth]
            below = rid >= r0 + 8
            mrows, wrows, cs = [], [], []
            for j in range(8):
                rs = lax.rsqrt(p[j][j:j + 1, :])
                pj = p[j] * rs
                cj = c[j] * rs
                mj = rm[j:j + 1] * jnp.tile(rs, (1, width // 128))
                wj = rw[j:j + 1] * jnp.tile(rs, (1, wwidth // 128))
                for k in range(j + 1, 8):
                    sc = pj[k:k + 1, :]
                    p[k] = p[k] - pj * sc
                    c[k] = c[k] - cj * sc
                pm = jnp.where(sub > j, pj, 0.0)
                rm = rm - jnp.tile(pm, (1, width // 128)) * mj
                rw = rw - jnp.tile(pm, (1, wwidth // 128)) * wj
                mrows.append(mj)
                wrows.append(wj)
                cs.append(jnp.where(below, cj, 0.0))
            w = w_ref[base:n, :wwidth]
            for j in range(8):
                m = m - jnp.tile(cs[j], (1, width // 128)) * mrows[j]
                w = w - jnp.tile(cs[j], (1, wwidth // 128)) * wrows[j]
            w_ref[base:n, :wwidth] = w
            w_ref[pl.ds(r0, 8), :wwidth] = jnp.concatenate(wrows, axis=0)
            m_ref[base:n, :width] = pltpu.roll(m, width - 8, 1)
            return carry

        lax.fori_loop(0, seg // 8, body, 0)

def finish_kernel(root, g_ref, s_ref, a_ref, m_ref, w_ref):
    n = g_ref.shape[0]
    m_ref[...] = g_ref[...]
    chol_steps(m_ref, w_ref, n, 4)
    basis = lax.dot_general(s_ref[...], w_ref[...], (((1,), (1,)), ((), ())), precision=HI, preferred_element_type=jnp.float32)
    a_ref[...] = (root * basis).astype(jnp.bfloat16)

def finish(gram, sample, root):
    n = gram.shape[0]
    return pl.pallas_call(functools.partial(finish_kernel, root),
        out_shape=jax.ShapeDtypeStruct(sample.shape, jnp.bfloat16),
        in_specs=[pl.BlockSpec(memory_space=pltpu.VMEM)] * 2,
        out_specs=pl.BlockSpec(memory_space=pltpu.VMEM),
        scratch_shapes=[pltpu.VMEM((n, n), jnp.float32)] * 2,
        compiler_params=pltpu.CompilerParams(vmem_limit_bytes=32 << 20))(gram, sample)


def copy_to(src, dst, send, recv, axis, index):
    return pltpu.make_async_remote_copy(
        src_ref=src, dst_ref=dst, send_sem=send, recv_sem=recv, device_id={axis: index}, device_id_type=MESH
    )


def greet(axes):
    barrier = pltpu.get_barrier_semaphore()
    count = 0
    for axis, size in axes:
        me = lax.axis_index(axis)
        for d in range(1, size):
            pl.semaphore_signal(barrier, inc=1, device_id={axis: lax.rem(me + d, size)}, device_id_type=MESH)
            count += 1
    pl.semaphore_wait(barrier, count)


def sample_kernel(
    n, nc, w_hbm, u_hbm, k_hbm, l_hbm, s_hbm, pe_ref, sample_ref, gram_ref,
    w_v, u_v, k_v, s_v, l_v, expand, own, recv_p, recv_s, send_p, send_s, acc, rs_recv, samp, gpart, gz, gfull,
    in_sem, l_sem, sp_sem, rp_sem, ss_sem, rsv_sem, a_send, a_recv, b_send, b_recv, c_send, c_recv, d_send, d_recv,
):
    r = lax.axis_index("rows")
    c = lax.axis_index("cols")
    rank = s_v.shape[1]
    block, depth = l_hbm.shape
    ck = block // NCHUNK
    local_rows, width = w_v.shape
    pe_steps = width // (8 * WORDS)
    nonzero = (c + 1) * block > r * depth
    has_p = r > 0
    has_s = jnp.logical_and(r < n - 1, (c + 1) * block > (r + 1) * depth)
    give_s = jnp.logical_and(r > 0, nonzero)
    rr = n - 1 - r

    def load(t):
        return pltpu.make_async_copy(l_hbm.at[pl.ds(pl.multiple_of(t * ck, ck), ck), :], l_v.at[lax.rem(t, 2)], l_sem.at[lax.rem(t, 2)])

    ins = [pltpu.make_async_copy(a, b, in_sem.at[i]) for i, (a, b) in enumerate(((s_hbm, s_v), (w_hbm, w_v), (u_hbm, u_v), (k_hbm, k_v)))]
    ins[0].start()

    @pl.when(nonzero)
    def _():
        load(0).start()

    for one in ins[1:]:
        one.start()
    word = lax.broadcasted_iota(jnp.int32, (WORDS, 8 * WORDS), 0)
    lane = lax.broadcasted_iota(jnp.int32, (WORDS, 8 * WORDS), 1)
    expand[...] = jnp.where(lax.shift_right_logical(lane, 3) == word, 1.0, 0.0).astype(BF16)
    acc[...] = jnp.zeros_like(acc)
    greet((("rows", n), ("cols", nc)))
    for one in ins:
        one.wait()

    def forward(j):
        return copy_to(send_p.at[j], recv_p.at[j], sp_sem.at[j], rp_sem.at[j], "rows", lax.rem(r + 1, n))

    def backward(j):
        return copy_to(send_s.at[j], recv_s.at[j], ss_sem.at[j], rsv_sem.at[j], "rows", lax.rem(r + n - 1, n))

    def step(t, carry):
        @pl.when(jnp.logical_and(t < NCHUNK, nonzero))
        def _():
            @pl.when(t + 1 < NCHUNK)
            def _():
                load(t + 1).start()

            load(t).wait()
            own[t] = jnp.dot(l_v[lax.rem(t, 2)], s_v[...], preferred_element_type=F32)

        @pl.when(jnp.logical_and(t < NCHUNK, jnp.logical_not(nonzero)))
        def _():
            own[t] = jnp.zeros((ck, rank), F32)

        p = t - r

        @pl.when(jnp.logical_and(p >= 0, p < NCHUNK))
        def _():
            @pl.when(has_p)
            def _():
                forward(p).wait_recv()

            @pl.when(r < n - 1)
            def _():
                @pl.when(has_p)
                def _():
                    send_p[p] = (own[p] + recv_p[p].astype(F32)).astype(BF16)

                @pl.when(jnp.logical_not(has_p))
                def _():
                    send_p[p] = own[p].astype(BF16)

                forward(p).start()

        s = t - rr

        @pl.when(jnp.logical_and(s >= 0, s < NCHUNK))
        def _():
            @pl.when(has_s)
            def _():
                backward(s).wait_recv()

            @pl.when(give_s)
            def _():
                @pl.when(has_s)
                def _():
                    send_s[s] = (own[s] + recv_s[s].astype(F32)).astype(BF16)

                @pl.when(jnp.logical_not(has_s))
                def _():
                    send_s[s] = own[s].astype(BF16)

                backward(s).start()

        @pl.when(t < pe_steps)
        def _():
            codes = k_v[:, pl.ds(pl.multiple_of(t * WORDS, WORDS), WORDS)]
            second = lax.shift_right_logical(codes * 43, 8)
            first = codes - 6 * second
            table = jnp.full(codes.shape, 0xCA6953, jnp.int32)
            low = lax.shift_right_logical(table, 4 * first) & 15
            high = lax.shift_right_logical(table, 4 * second) & 15
            packed = (low + 16 * high).astype(F32).astype(BF16)
            spread = jnp.dot(packed, expand[...], preferred_element_type=F32).astype(jnp.int32)
            bit = jnp.left_shift(1, lax.broadcasted_iota(jnp.int32, spread.shape, 1) & 7)
            at = pl.ds(pl.multiple_of(t * 8 * WORDS, 8 * WORDS), 8 * WORDS)
            wv = w_v[:, at].astype(F32)
            uv = u_v[:, at].astype(F32)
            pe_ref[:, at] = (wv - jnp.where((spread & bit) != 0, wv + uv, 0.0)).astype(BF16)

        m = t - jnp.maximum(r, rr)

        @pl.when(jnp.logical_and(m >= 0, m < NCHUNK))
        def _():
            @pl.when(has_p)
            def _():
                own[m] = own[m] + recv_p[m].astype(F32)

            @pl.when(has_s)
            def _():
                own[m] = own[m] + recv_s[m].astype(F32)

            part = jnp.dot(pe_ref[:, pl.ds(pl.multiple_of(m * ck, ck), ck)], own[m].astype(BF16), preferred_element_type=F32)
            acc[...] += part.reshape(acc.shape)

        return carry

    lax.fori_loop(0, NCHUNK + n - 1, step, 0)

    def drain(j, carry):
        @pl.when(r < n - 1)
        def _():
            forward(j).wait_send()

        @pl.when(give_s)
        def _():
            backward(j).wait_send()

        return carry

    def peers(size, me):
        return [lax.rem(me + d, size) for d in range(1, size)]

    def swap(copies_out, copies_in):
        for one in copies_out:
            one.start()
        for one in copies_in:
            one.wait_recv()

    def exchange(src_of, dst, send, recv, axis, size, me):
        out = [copy_to(src_of(p), dst.at[me], send.at[p], recv.at[me], axis, p) for p in peers(size, me)]
        back = [copy_to(src_of(p), dst.at[p], send.at[p], recv.at[p], axis, p) for p in peers(size, me)]
        swap(out, back)
        return out

    sent = exchange(lambda p: acc.at[p], rs_recv, a_send, a_recv, "cols", nc, c)
    total = acc[c]
    for p in peers(nc, c):
        total = total + rs_recv[p]
    samp[c] = total
    sent += exchange(lambda p: samp.at[c], samp, b_send, b_recv, "cols", nc, c)
    sample = samp[...].reshape(local_rows, rank)
    sample_ref[...] = sample
    gpart[...] = lax.dot_general(
        sample, sample, (((0,), (0,)), ((), ())), precision=HI, preferred_element_type=F32
    ).reshape(gpart.shape)
    sent += exchange(lambda p: gpart.at[c], gz, c_send, c_recv, "rows", n, r)
    total = gpart[c]
    for p in peers(n, r):
        total = total + gz[p]
    gfull[c] = total
    sent += exchange(lambda p: gfull.at[c], gfull, d_send, d_recv, "cols", nc, c)
    gram_ref[...] = gfull[...].reshape(rank, rank)
    lax.fori_loop(0, NCHUNK, drain, 0)
    for one in sent:
        one.wait_send()


def sample_and_gram(n, nc, weight, update, codes, factor, sketch):
    rows, width = weight.shape
    block, depth = factor.shape
    rank = sketch.shape[1]
    ck = block // NCHUNK
    chunks = (NCHUNK, ck, rank)
    vm = pl.BlockSpec(memory_space=pltpu.VMEM)
    dma = pltpu.SemaphoreType.DMA
    return pl.pallas_call(
        functools.partial(sample_kernel, n, nc),
        out_shape=(
            jax.ShapeDtypeStruct((rows, width), BF16),
            jax.ShapeDtypeStruct((rows, rank), F32),
            jax.ShapeDtypeStruct((rank, rank), F32),
        ),
        in_specs=[pl.BlockSpec(memory_space=pl.ANY)] * 5,
        out_specs=(vm, vm, vm),
        scratch_shapes=[
            pltpu.VMEM((rows, width), BF16),
            pltpu.VMEM((rows, width), BF16),
            pltpu.VMEM(codes.shape, jnp.int32),
            pltpu.VMEM(sketch.shape, BF16),
            pltpu.VMEM((2, ck, depth), BF16),
            pltpu.VMEM((WORDS, 8 * WORDS), BF16),
            pltpu.VMEM(chunks, F32),
            pltpu.VMEM(chunks, BF16),
            pltpu.VMEM(chunks, BF16),
            pltpu.VMEM(chunks, BF16),
            pltpu.VMEM(chunks, BF16),
            pltpu.VMEM((nc, rows // nc, rank), F32),
            pltpu.VMEM((nc, rows // nc, rank), F32),
            pltpu.VMEM((nc, rows // nc, rank), F32),
            pltpu.VMEM((nc, rank // nc, rank), F32),
            pltpu.VMEM((n, rank // nc, rank), F32),
            pltpu.VMEM((nc, rank // nc, rank), F32),
            dma((4,)),
            dma((2,)),
            dma((NCHUNK,)),
            dma((NCHUNK,)),
            dma((NCHUNK,)),
            dma((NCHUNK,)),
            dma((nc,)),
            dma((nc,)),
            dma((nc,)),
            dma((nc,)),
            dma((n,)),
            dma((n,)),
            dma((nc,)),
            dma((nc,)),
        ],
        compiler_params=pltpu.CompilerParams(collective_id=0, has_side_effects=True, vmem_limit_bytes=52 << 20),
        name="sample_and_gram",
    )(weight, update, codes, factor, sketch)


def second_kernel(n, q_count, root, a_ref, pe_ref, out_ref, own, recv_p, recv_s, send_p, send_s, sp_sem, rp_sem, ss_sem, rs_sem):
    r = lax.axis_index("rows")
    rr = n - 1 - r
    share, width = out_ref.shape
    cq = width // q_count
    items = (n - 1) * q_count
    a_t = a_ref[...]

    def fill(q, carry):
        at = pl.ds(pl.multiple_of(q * cq, cq), cq)
        part = lax.dot_general(a_t, pe_ref[:, at], (((0,), (0,)), ((), ())), preferred_element_type=F32)
        own[:, :, at] = part.reshape(n, share, cq)
        return carry

    lax.fori_loop(0, q_count, fill, 0)
    greet((("rows", n),))

    def forward(e):
        return copy_to(send_p.at[e], recv_p.at[e], sp_sem.at[e], rp_sem.at[e], "rows", lax.rem(r + 1, n))

    def backward(e):
        return copy_to(send_s.at[e], recv_s.at[e], ss_sem.at[e], rs_sem.at[e], "rows", lax.rem(r + n - 1, n))

    def pass_on(e, place, target, t, copy, recv, send):
        at = pl.ds(pl.multiple_of((e % q_count) * cq, cq), cq)

        @pl.when(jnp.logical_and(place > 0, place <= target))
        def _():
            copy(e).wait_recv()
            own[t, :, at] = own[t, :, at] + recv[e].astype(F32)

        @pl.when(place < target)
        def _():
            send[e] = own[t, :, at].astype(BF16)
            copy(e).start()

    def step(tau, carry):
        e = tau - r

        @pl.when(jnp.logical_and(e >= 0, e < items))
        def _():
            target = n - 1 - e // q_count
            pass_on(e, r, target, target, forward, recv_p, send_p)

        f = tau - rr

        @pl.when(jnp.logical_and(f >= 0, f < items))
        def _():
            target = n - 1 - f // q_count
            pass_on(f, rr, target, n - 1 - target, backward, recv_s, send_s)

        return carry

    lax.fori_loop(0, items + n - 1, step, 0)

    def drain(e, carry):
        target = n - 1 - e // q_count

        @pl.when(r < target)
        def _():
            forward(e).wait_send()

        @pl.when(rr < target)
        def _():
            backward(e).wait_send()

        return carry

    out_ref[...] = (own[r] * (1.0 / root)).astype(BF16)
    lax.fori_loop(0, items, drain, 0)


def second_factor(n, root, a, pe):
    rank = a.shape[1]
    width = pe.shape[1]
    q_count = max(1, 16 // n)
    items = ((n - 1) * q_count, rank // n, width // q_count)
    vm = pl.BlockSpec(memory_space=pltpu.VMEM)
    dma = pltpu.SemaphoreType.DMA
    return pl.pallas_call(
        functools.partial(second_kernel, n, q_count, root),
        out_shape=jax.ShapeDtypeStruct((rank // n, width), BF16),
        in_specs=[vm, vm],
        out_specs=vm,
        scratch_shapes=[pltpu.VMEM((n, rank // n, width), F32)]
        + [pltpu.VMEM(items, BF16)] * 4
        + [dma((items[0],))] * 4,
        compiler_params=pltpu.CompilerParams(collective_id=1, has_side_effects=True, vmem_limit_bytes=48 << 20),
        name="second_factor",
    )(a, pe)


def shards(n, nc, weight, update, keep_codes, chol_factor, sketch):
    root = math.sqrt(weight.shape[0] * n)
    pe, sample, gram = sample_and_gram(n, nc, weight, update, keep_codes, chol_factor, sketch)
    adapter_a = finish(gram, sample, root)
    return (adapter_a, second_factor(n, root, adapter_a, pe))


def solution(mesh):
    in_specs = (
        P(("layers", "rows"), "cols"),
        P(("layers", "rows"), "cols"),
        P(("layers", "rows"), "cols"),
        P(("layers", "cols"), "rows"),
        P("rows", None),
    )
    out_specs = (P(("layers", "rows"), None), P(("layers", "rows"), "cols"))
    body = functools.partial(shards, mesh.shape["rows"], mesh.shape["cols"])
    return jax.shard_map(body, mesh=mesh, in_specs=in_specs, out_specs=out_specs, check_vma=False)
```

```python
import functools
import math

import jax
import jax.numpy as jnp
from jax import lax
from jax.experimental import pallas as pl
from jax.experimental.pallas import tpu as pltpu
from jax.sharding import PartitionSpec as P

MESH = pl.DeviceIdType.MESH
F32 = jnp.float32
BF16 = jnp.bfloat16
NCHUNK = 32
SUBS = 4
LAG = 3
GATHER = 3
WORDS = 128

HI = lax.Precision.HIGHEST

def chol_steps(m_ref, w_ref, n, nseg):
    row = lax.broadcasted_iota(jnp.int32, (n, n), 0)
    col = lax.broadcasted_iota(jnp.int32, (n, n), 1)
    w_ref[...] = jnp.where(row == col, 1.0, 0.0).astype(jnp.float32)
    seg = n // nseg
    sub = lax.broadcasted_iota(jnp.int32, (8, 128), 0)
    for s in range(nseg):
        base = s * seg
        rows = n - base
        width = max(128, -(-rows // 128) * 128)
        wwidth = max(128, -(-(base + seg) // 128) * 128)
        rid = lax.broadcasted_iota(jnp.int32, (rows, 128), 0) + base

        def body(i, carry, base=base, rows=rows, width=width, wwidth=wwidth, rid=rid):
            r0 = pl.multiple_of(base + i * 8, 8)
            m = m_ref[base:n, :width]
            c = [jnp.broadcast_to(m[:, j:j + 1], (rows, 128)) for j in range(8)]
            b8 = m_ref[pl.ds(r0, 8), 0:128]
            p = [jnp.broadcast_to(b8[:, j:j + 1], (8, 128)) for j in range(8)]
            rm = m_ref[pl.ds(r0, 8), :width]
            rw = w_ref[pl.ds(r0, 8), :wwidth]
            below = rid >= r0 + 8
            mrows, wrows, cs = [], [], []
            for j in range(8):
                rs = lax.rsqrt(p[j][j:j + 1, :])
                pj = p[j] * rs
                cj = c[j] * rs
                mj = rm[j:j + 1] * jnp.tile(rs, (1, width // 128))
                wj = rw[j:j + 1] * jnp.tile(rs, (1, wwidth // 128))
                for k in range(j + 1, 8):
                    sc = pj[k:k + 1, :]
                    p[k] = p[k] - pj * sc
                    c[k] = c[k] - cj * sc
                pm = jnp.where(sub > j, pj, 0.0)
                rm = rm - jnp.tile(pm, (1, width // 128)) * mj
                rw = rw - jnp.tile(pm, (1, wwidth // 128)) * wj
                mrows.append(mj)
                wrows.append(wj)
                cs.append(jnp.where(below, cj, 0.0))
            w = w_ref[base:n, :wwidth]
            for j in range(8):
                m = m - jnp.tile(cs[j], (1, width // 128)) * mrows[j]
                w = w - jnp.tile(cs[j], (1, wwidth // 128)) * wrows[j]
            w_ref[base:n, :wwidth] = w
            w_ref[pl.ds(r0, 8), :wwidth] = jnp.concatenate(wrows, axis=0)
            m_ref[base:n, :width] = pltpu.roll(m, width - 8, 1)
            return carry

        lax.fori_loop(0, seg // 8, body, 0)

def copy_to(src, dst, send, recv, axis, index):
    return pltpu.make_async_remote_copy(
        src_ref=src, dst_ref=dst, send_sem=send, recv_sem=recv, device_id={axis: index}, device_id_type=MESH
    )


def greet(axes):
    barrier = pltpu.get_barrier_semaphore()
    count = 0
    for axis, size in axes:
        me = lax.axis_index(axis)
        for d in range(1, size):
            pl.semaphore_signal(barrier, inc=1, device_id={axis: lax.rem(me + d, size)}, device_id_type=MESH)
            count += 1
    pl.semaphore_wait(barrier, count)


def whole_kernel(
    n, nc, q_count, gq, root, w_hbm, u_hbm, k_hbm, l_hbm, s_hbm, a_ref, out_ref, pe_ref,
    w_v, u_v, k_v, s_v, l_v, expand, own, recv_p, recv_s, send_p, send_s, acc, rs_recv, samp, gpart, gz, gfull,
    in_sem, l_sem, sp_sem, rp_sem, ss_sem, rsv_sem, a_send, a_recv, b_send, b_recv, c_send, c_recv, d_send, d_recv,
    m_ref, inv_ref, a_l, a_r, pe_l, pe_r, own2, own_l, own_r, q_recv_p, q_recv_s, q_send_p, q_send_s,
    qsp_sem, qrp_sem, qss_sem, qrs_sem, n_send, n_recv,
):
    r = lax.axis_index("rows")
    c = lax.axis_index("cols")
    rank = s_v.shape[1]
    block, depth = l_hbm.shape
    ck = block // NCHUNK
    local_rows, width = w_v.shape
    pe_steps = width // (8 * WORDS)
    nonzero = (c + 1) * block > r * depth
    has_p = r > 0
    has_s = jnp.logical_and(r < n - 1, (c + 1) * block > (r + 1) * depth)
    give_s = jnp.logical_and(r > 0, nonzero)
    rr = n - 1 - r

    big = SUBS * ck

    def load(t):
        return pltpu.make_async_copy(l_hbm.at[pl.ds(pl.multiple_of(t * big, big), big), :], l_v.at[lax.rem(t, 2)], l_sem.at[lax.rem(t, 2)])

    ins = [pltpu.make_async_copy(a, b, in_sem.at[i]) for i, (a, b) in enumerate(((s_hbm, s_v), (w_hbm, w_v), (u_hbm, u_v), (k_hbm, k_v)))]
    ins[0].start()

    @pl.when(nonzero)
    def _():
        load(0).start()

    for one in ins[1:]:
        one.start()
    word = lax.broadcasted_iota(jnp.int32, (WORDS, 8 * WORDS), 0)
    lane = lax.broadcasted_iota(jnp.int32, (WORDS, 8 * WORDS), 1)
    expand[...] = jnp.where(lax.shift_right_logical(lane, 3) == word, 1.0, 0.0).astype(BF16)
    acc[...] = jnp.zeros_like(acc)
    greet((("rows", n), ("cols", nc)))
    for one in ins:
        one.wait()

    def forward(j):
        return copy_to(send_p.at[j], recv_p.at[j], sp_sem.at[j], rp_sem.at[j], "rows", lax.rem(r + 1, n))

    def backward(j):
        return copy_to(send_s.at[j], recv_s.at[j], ss_sem.at[j], rsv_sem.at[j], "rows", lax.rem(r + n - 1, n))

    def whiten(t):
        at = pl.ds(pl.multiple_of(t * SUBS, SUBS), SUBS)

        @pl.when(nonzero)
        def _():
            @pl.when((t + 1) * SUBS < NCHUNK)
            def _():
                load(t + 1).start()

            load(t).wait()
            own[at] = jnp.dot(l_v[lax.rem(t, 2)], s_v[...], preferred_element_type=F32).reshape(SUBS, ck, rank)

        @pl.when(jnp.logical_not(nonzero))
        def _():
            own[at] = jnp.zeros((SUBS, ck, rank), F32)

    def step(t, carry):
        @pl.when(jnp.logical_and(t % SUBS == 0, t < NCHUNK))
        def _():
            whiten(t // SUBS)

        p = t - LAG * r

        @pl.when(jnp.logical_and(p >= 0, p < NCHUNK))
        def _():
            @pl.when(has_p)
            def _():
                forward(p).wait_recv()

            @pl.when(r < n - 1)
            def _():
                @pl.when(has_p)
                def _():
                    send_p[p] = (own[p] + recv_p[p].astype(F32)).astype(BF16)

                @pl.when(jnp.logical_not(has_p))
                def _():
                    send_p[p] = own[p].astype(BF16)

                forward(p).start()

        s = t - LAG * rr

        @pl.when(jnp.logical_and(s >= 0, s < NCHUNK))
        def _():
            @pl.when(has_s)
            def _():
                backward(s).wait_recv()

            @pl.when(give_s)
            def _():
                @pl.when(has_s)
                def _():
                    send_s[s] = (own[s] + recv_s[s].astype(F32)).astype(BF16)

                @pl.when(jnp.logical_not(has_s))
                def _():
                    send_s[s] = own[s].astype(BF16)

                backward(s).start()

        @pl.when(jnp.logical_and(t % SUBS == 1, t < pe_steps * SUBS))
        def _():
            i = t // SUBS
            codes = k_v[:, pl.ds(pl.multiple_of(i * WORDS, WORDS), WORDS)]
            second = lax.shift_right_logical(codes * 43, 8)
            first = codes - 6 * second
            table = jnp.full(codes.shape, 0xCA6953, jnp.int32)
            low = lax.shift_right_logical(table, 4 * first) & 15
            high = lax.shift_right_logical(table, 4 * second) & 15
            packed = (low + 16 * high).astype(F32).astype(BF16)
            spread = jnp.dot(packed, expand[...], preferred_element_type=F32).astype(jnp.int32)
            bit = jnp.left_shift(1, lax.broadcasted_iota(jnp.int32, spread.shape, 1) & 7)
            at = pl.ds(pl.multiple_of(i * 8 * WORDS, 8 * WORDS), 8 * WORDS)
            wv = w_v[:, at].astype(F32)
            uv = u_v[:, at].astype(F32)
            pe_ref[:, at] = (wv - jnp.where((spread & bit) != 0, wv + uv, 0.0)).astype(BF16)

        m = t - LAG * jnp.maximum(r, rr)

        @pl.when(jnp.logical_and(m >= 0, m < NCHUNK))
        def _():
            @pl.when(has_p)
            def _():
                own[m] = own[m] + recv_p[m].astype(F32)

            @pl.when(has_s)
            def _():
                own[m] = own[m] + recv_s[m].astype(F32)

            @pl.when(m % SUBS == SUBS - 1)
            def _():
                i = m // SUBS
                whole = own[pl.ds(pl.multiple_of(i * SUBS, SUBS), SUBS)].reshape(big, rank).astype(BF16)
                part = jnp.dot(pe_ref[:, pl.ds(pl.multiple_of(i * big, big), big)], whole, preferred_element_type=F32)
                acc[...] += part.reshape(acc.shape)

        return carry

    lax.fori_loop(0, NCHUNK + LAG * (n - 1), step, 0)

    def drain(j, carry):
        @pl.when(r < n - 1)
        def _():
            forward(j).wait_send()

        @pl.when(give_s)
        def _():
            backward(j).wait_send()

        return carry

    def peers(size, me):
        return [lax.rem(me + d, size) for d in range(1, size)]

    def swap(copies_out, copies_in):
        for one in copies_out:
            one.start()
        for one in copies_in:
            one.wait_recv()

    def exchange(src_of, dst, send, recv, axis, size, me):
        out = [copy_to(src_of(p), dst.at[me], send.at[p], recv.at[me], axis, p) for p in peers(size, me)]
        back = [copy_to(src_of(p), dst.at[p], send.at[p], recv.at[p], axis, p) for p in peers(size, me)]
        swap(out, back)
        return out

    sent = exchange(lambda p: acc.at[p], rs_recv, a_send, a_recv, "cols", nc, c)
    total = acc[c]
    for p in peers(nc, c):
        total = total + rs_recv[p]
    samp[c] = total
    sent += exchange(lambda p: samp.at[c], samp, b_send, b_recv, "cols", nc, c)
    sample = samp[...].reshape(local_rows, rank)
    gpart[...] = lax.dot_general(
        sample, sample, (((0,), (0,)), ((), ())), precision=HI, preferred_element_type=F32
    ).reshape(gpart.shape)
    sent += exchange(lambda p: gpart.at[c], gz, c_send, c_recv, "rows", n, r)
    total = gpart[c]
    for p in peers(n, r):
        total = total + gz[p]
    gfull[c] = total
    sent += exchange(lambda p: gfull.at[c], gfull, d_send, d_recv, "cols", nc, c)
    share, cq = out_ref.shape[0], width // q_count
    gw = gq * cq
    nq = q_count - gq
    plain = (n - 1) * nq
    lo, hi = lax.rem(r + n - 1, n), lax.rem(r + 1, n)
    near = [
        copy_to(pe_ref.at[:, 0:gw], pe_l, n_send.at[0], n_recv.at[0], "rows", hi),
        copy_to(pe_ref.at[:, 0:gw], pe_r, n_send.at[1], n_recv.at[1], "rows", lo),
        copy_to(a_ref, a_l, n_send.at[2], n_recv.at[2], "rows", hi),
        copy_to(a_ref, a_r, n_send.at[3], n_recv.at[3], "rows", lo),
    ]

    def start_near(i):
        @pl.when(r < n - 1)
        def _():
            near[i].start()

        @pl.when(r > 0)
        def _():
            near[i + 1].start()

    start_near(0)
    m_ref[...] = gfull[...].reshape(rank, rank)
    chol_steps(m_ref, inv_ref, rank, 4)
    basis = lax.dot_general(sample, inv_ref[...], (((1,), (1,)), ((), ())), precision=HI, preferred_element_type=F32)
    a_ref[...] = (root * basis).astype(BF16)
    start_near(2)

    def times(a, pe, at):
        return lax.dot_general(a[...], pe[:, at], (((0,), (0,)), ((), ())), preferred_element_type=F32).reshape(n, share, cq)

    def column(q):
        return pl.ds(pl.multiple_of(q * cq, cq), cq)

    def fill(i, carry):
        at = column(q_count - 1 - i)
        own2[:, :, at] = times(a_ref, pe_ref, at)
        return carry

    lax.fori_loop(0, q_count, fill, 0)

    def q_forward(b):
        return copy_to(q_send_p.at[b], q_recv_p.at[b], qsp_sem.at[b], qrp_sem.at[b], "rows", hi)

    def q_backward(b):
        return copy_to(q_send_s.at[b], q_recv_s.at[b], qss_sem.at[b], qrs_sem.at[b], "rows", lo)

    def first_sends(e, carry):
        at = column(gq + e % nq)

        @pl.when(r == 0)
        def _():
            q_send_p[e] = own2[n - 1 - e // nq, :, at].astype(BF16)
            q_forward(e).start()

        @pl.when(rr == 0)
        def _():
            q_send_s[e] = own2[e // nq, :, at].astype(BF16)
            q_backward(e).start()

        return carry

    lax.fori_loop(0, plain, first_sends, 0)

    def pass_on(b, first, least, place, target, t, base, at, copy, recv, send):
        @pl.when(jnp.logical_and(place > first, place <= target))
        def _():
            copy(b).wait_recv()
            base[t, :, at] = base[t, :, at] + recv[b].astype(F32)

        @pl.when(jnp.logical_and(place >= least, place < target))
        def _():
            send[b] = base[t, :, at].astype(BF16)
            copy(b).start()

    def chain(count, per, q0, b0, first, least, base_p, base_s):
        def step2(tau, carry):
            e = tau - LAG * r

            @pl.when(jnp.logical_and(e >= 0, e < count))
            def _():
                target = n - 1 - e // per
                pass_on(b0 + e, first, least, r, target, target, base_p, column(q0 + e % per), q_forward, q_recv_p, q_send_p)

            f = tau - LAG * rr

            @pl.when(jnp.logical_and(f >= 0, f < count))
            def _():
                target = n - 1 - f // per
                pass_on(b0 + f, first, least, rr, target, n - 1 - target, base_s, column(q0 + f % per), q_backward, q_recv_s, q_send_s)

            return carry

        lax.fori_loop(0, count + LAG * (n - 1), step2, 0)

    @pl.when(r > 0)
    def _():
        near[0].wait_recv()
        near[2].wait_recv()
        for q in range(gq):
            own_l[:, :, q * cq:(q + 1) * cq] = times(a_l, pe_l, slice(q * cq, (q + 1) * cq))

    @pl.when(r < n - 1)
    def _():
        near[1].wait_recv()
        near[3].wait_recv()
        for q in range(gq):
            own_r[:, :, q * cq:(q + 1) * cq] = times(a_r, pe_r, slice(q * cq, (q + 1) * cq))

    chain((n - 1) * gq, gq, 0, plain, 1, 1, own_l, own_r)
    chain(plain, nq, gq, 0, 0, 1, own2, own2)

    @pl.when(r > 0)
    def _():
        own2[r, :, 0:gw] = own2[r, :, 0:gw] + own_l[r]

    @pl.when(r < n - 1)
    def _():
        own2[r, :, 0:gw] = own2[r, :, 0:gw] + own_r[r]

    out_ref[...] = (own2[r] * (1.0 / root)).astype(BF16)

    lax.fori_loop(0, NCHUNK, drain, 0)

    def drain_second(count, per, b0, first):
        def one_drain(e, carry):
            target = n - 1 - e // per

            @pl.when(jnp.logical_and(r >= first, r < target))
            def _():
                q_forward(b0 + e).wait_send()

            @pl.when(jnp.logical_and(rr >= first, rr < target))
            def _():
                q_backward(b0 + e).wait_send()

            return carry

        lax.fori_loop(0, count, one_drain, 0)

    drain_second(plain, nq, 0, 0)
    drain_second((n - 1) * gq, gq, plain, 1)

    @pl.when(r < n - 1)
    def _():
        near[0].wait_send()
        near[2].wait_send()

    @pl.when(r > 0)
    def _():
        near[1].wait_send()
        near[3].wait_send()

    for one in sent:
        one.wait_send()


def adapters(n, nc, root, weight, update, codes, factor, sketch):
    rows, width = weight.shape
    block, depth = factor.shape
    rank = sketch.shape[1]
    ck = block // NCHUNK
    chunks = (NCHUNK, ck, rank)
    q_count = max(2, 32 // n)
    gq = max(1, q_count * GATHER // 8)
    gw = gq * (width // q_count)
    items = ((n - 1) * q_count, rank // n, width // q_count)
    vm = pl.BlockSpec(memory_space=pltpu.VMEM)
    dma = pltpu.SemaphoreType.DMA
    return pl.pallas_call(
        functools.partial(whole_kernel, n, nc, q_count, gq, root),
        out_shape=(jax.ShapeDtypeStruct((rows, rank), BF16), jax.ShapeDtypeStruct((rank // n, width), BF16)),
        in_specs=[pl.BlockSpec(memory_space=pl.ANY)] * 5,
        out_specs=(vm, vm),
        scratch_shapes=[
            pltpu.VMEM((rows, width), BF16),
            pltpu.VMEM((rows, width), BF16),
            pltpu.VMEM((rows, width), BF16),
            pltpu.VMEM(codes.shape, jnp.int32),
            pltpu.VMEM(sketch.shape, BF16),
            pltpu.VMEM((2, SUBS * ck, depth), BF16),
            pltpu.VMEM((WORDS, 8 * WORDS), BF16),
            pltpu.VMEM(chunks, F32),
            pltpu.VMEM(chunks, BF16),
            pltpu.VMEM(chunks, BF16),
            pltpu.VMEM(chunks, BF16),
            pltpu.VMEM(chunks, BF16),
            pltpu.VMEM((nc, rows // nc, rank), F32),
            pltpu.VMEM((nc, rows // nc, rank), F32),
            pltpu.VMEM((nc, rows // nc, rank), F32),
            pltpu.VMEM((nc, rank // nc, rank), F32),
            pltpu.VMEM((n, rank // nc, rank), F32),
            pltpu.VMEM((nc, rank // nc, rank), F32),
            dma((4,)),
            dma((2,)),
            dma((NCHUNK,)),
            dma((NCHUNK,)),
            dma((NCHUNK,)),
            dma((NCHUNK,)),
            dma((nc,)),
            dma((nc,)),
            dma((nc,)),
            dma((nc,)),
            dma((n,)),
            dma((n,)),
            dma((nc,)),
            dma((nc,)),
            pltpu.VMEM((rank, rank), F32),
            pltpu.VMEM((rank, rank), F32),
            pltpu.VMEM((rows, rank), BF16),
            pltpu.VMEM((rows, rank), BF16),
            pltpu.VMEM((rows, gw), BF16),
            pltpu.VMEM((rows, gw), BF16),
            pltpu.VMEM((n, rank // n, width), F32),
            pltpu.VMEM((n, rank // n, gw), F32),
            pltpu.VMEM((n, rank // n, gw), F32),
        ]
        + [pltpu.VMEM(items, BF16)] * 4
        + [dma((items[0],))] * 4
        + [dma((4,))] * 2,
        compiler_params=pltpu.CompilerParams(collective_id=0, has_side_effects=True, vmem_limit_bytes=58 << 20),
        name="adapters",
    )(weight, update, codes, factor, sketch)


def shards(n, nc, weight, update, keep_codes, chol_factor, sketch):
    root = math.sqrt(weight.shape[0] * n)
    return adapters(n, nc, root, weight, update, keep_codes, chol_factor, sketch)


def solution(mesh):
    in_specs = (
        P(("layers", "rows"), "cols"),
        P(("layers", "rows"), "cols"),
        P(("layers", "rows"), "cols"),
        P(("layers", "cols"), "rows"),
        P("rows", None),
    )
    out_specs = (P(("layers", "rows"), None), P(("layers", "rows"), "cols"))
    body = functools.partial(shards, mesh.shape["rows"], mesh.shape["cols"])
    return jax.shard_map(body, mesh=mesh, in_specs=in_specs, out_specs=out_specs, check_vma=False)
```

```python
import functools
import math

import jax
import jax.numpy as jnp
from jax import lax
from jax.experimental import pallas as pl
from jax.experimental.pallas import tpu as pltpu
from jax.sharding import PartitionSpec as P

MESH = pl.DeviceIdType.MESH
F32 = jnp.float32
BF16 = jnp.bfloat16
NCHUNK = 32
SUBS = 4
LAG = 3
GATHER = 3
WORDS = 128

HI = lax.Precision.HIGHEST

def chol_steps(m_ref, w_ref, n, nseg):
    row = lax.broadcasted_iota(jnp.int32, (n, n), 0)
    col = lax.broadcasted_iota(jnp.int32, (n, n), 1)
    w_ref[...] = jnp.where(row == col, 1.0, 0.0).astype(jnp.float32)
    seg = n // nseg
    sub = lax.broadcasted_iota(jnp.int32, (8, 128), 0)
    for s in range(nseg):
        base = s * seg
        rows = n - base
        width = max(128, -(-rows // 128) * 128)
        wwidth = max(128, -(-(base + seg) // 128) * 128)
        rid = lax.broadcasted_iota(jnp.int32, (rows, 128), 0) + base

        def body(i, carry, base=base, rows=rows, width=width, wwidth=wwidth, rid=rid):
            r0 = pl.multiple_of(base + i * 8, 8)
            m = m_ref[base:n, :width]
            c = [jnp.broadcast_to(m[:, j:j + 1], (rows, 128)) for j in range(8)]
            b8 = m_ref[pl.ds(r0, 8), 0:128]
            p = [jnp.broadcast_to(b8[:, j:j + 1], (8, 128)) for j in range(8)]
            rm = m_ref[pl.ds(r0, 8), :width]
            rw = w_ref[pl.ds(r0, 8), :wwidth]
            below = rid >= r0 + 8
            mrows, wrows, cs = [], [], []
            for j in range(8):
                rs = lax.rsqrt(p[j][j:j + 1, :])
                pj = p[j] * rs
                cj = c[j] * rs
                mj = rm[j:j + 1] * jnp.tile(rs, (1, width // 128))
                wj = rw[j:j + 1] * jnp.tile(rs, (1, wwidth // 128))
                for k in range(j + 1, 8):
                    sc = pj[k:k + 1, :]
                    p[k] = p[k] - pj * sc
                    c[k] = c[k] - cj * sc
                pm = jnp.where(sub > j, pj, 0.0)
                rm = rm - jnp.tile(pm, (1, width // 128)) * mj
                rw = rw - jnp.tile(pm, (1, wwidth // 128)) * wj
                mrows.append(mj)
                wrows.append(wj)
                cs.append(jnp.where(below, cj, 0.0))
            w = w_ref[base:n, :wwidth]
            for j in range(8):
                m = m - jnp.tile(cs[j], (1, width // 128)) * mrows[j]
                w = w - jnp.tile(cs[j], (1, wwidth // 128)) * wrows[j]
            w_ref[base:n, :wwidth] = w
            w_ref[pl.ds(r0, 8), :wwidth] = jnp.concatenate(wrows, axis=0)
            m_ref[base:n, :width] = pltpu.roll(m, width - 8, 1)
            return carry

        lax.fori_loop(0, seg // 8, body, 0)

def copy_to(src, dst, send, recv, axis, index):
    return pltpu.make_async_remote_copy(
        src_ref=src, dst_ref=dst, send_sem=send, recv_sem=recv, device_id={axis: index}, device_id_type=MESH
    )


def greet(axes):
    barrier = pltpu.get_barrier_semaphore()
    count = 0
    for axis, size in axes:
        me = lax.axis_index(axis)
        for d in range(1, size):
            pl.semaphore_signal(barrier, inc=1, device_id={axis: lax.rem(me + d, size)}, device_id_type=MESH)
            count += 1
    pl.semaphore_wait(barrier, count)


def whole_kernel(
    n, nc, q_count, gq, root, w_hbm, u_hbm, k_hbm, l_hbm, s_hbm, a_ref, out_ref, pe_ref,
    w_v, u_v, k_v, s_v, l_v, expand, own, recv_p, recv_s, send_p, send_s, acc, rs_recv, samp, gpart, gz, gfull,
    in_sem, l_sem, sp_sem, rp_sem, ss_sem, rsv_sem, a_send, a_recv, b_send, b_recv, c_send, c_recv, d_send, d_recv,
    m_ref, inv_ref, a_l, a_r, pe_l, pe_r, own2, own_l, own_r, q_recv_p, q_recv_s, q_send_p, q_send_s,
    qsp_sem, qrp_sem, qss_sem, qrs_sem, n_send, n_recv,
):
    r = lax.axis_index("rows")
    c = lax.axis_index("cols")
    rank = s_v.shape[1]
    block, depth = l_hbm.shape
    ck = block // NCHUNK
    local_rows, width = w_v.shape
    pe_steps = width // (8 * WORDS)
    nonzero = (c + 1) * block > r * depth
    has_p = r > 0
    has_s = jnp.logical_and(r < n - 1, (c + 1) * block > (r + 1) * depth)
    give_s = jnp.logical_and(r > 0, nonzero)
    rr = n - 1 - r

    big = SUBS * ck

    def load(t):
        return pltpu.make_async_copy(l_hbm.at[pl.ds(pl.multiple_of(t * big, big), big), :], l_v.at[lax.rem(t, 2)], l_sem.at[lax.rem(t, 2)])

    ins = [pltpu.make_async_copy(a, b, in_sem.at[i]) for i, (a, b) in enumerate(((s_hbm, s_v), (w_hbm, w_v), (u_hbm, u_v), (k_hbm, k_v)))]
    ins[0].start()

    @pl.when(nonzero)
    def _():
        load(0).start()

    for one in ins[1:]:
        one.start()
    word = lax.broadcasted_iota(jnp.int32, (WORDS, 8 * WORDS), 0)
    lane = lax.broadcasted_iota(jnp.int32, (WORDS, 8 * WORDS), 1)
    expand[...] = jnp.where(lax.shift_right_logical(lane, 3) == word, 1.0, 0.0).astype(BF16)
    acc[...] = jnp.zeros_like(acc)
    greet((("rows", n), ("cols", nc)))
    for one in ins:
        one.wait()

    def forward(j):
        return copy_to(send_p.at[j], recv_p.at[j], sp_sem.at[j], rp_sem.at[j], "rows", lax.rem(r + 1, n))

    def backward(j):
        return copy_to(send_s.at[j], recv_s.at[j], ss_sem.at[j], rsv_sem.at[j], "rows", lax.rem(r + n - 1, n))

    def whiten(t):
        at = pl.ds(pl.multiple_of(t * SUBS, SUBS), SUBS)

        @pl.when(nonzero)
        def _():
            @pl.when((t + 1) * SUBS < NCHUNK)
            def _():
                load(t + 1).start()

            load(t).wait()
            own[at] = jnp.dot(l_v[lax.rem(t, 2)], s_v[...], preferred_element_type=F32).reshape(SUBS, ck, rank)

        @pl.when(jnp.logical_not(nonzero))
        def _():
            own[at] = jnp.zeros((SUBS, ck, rank), F32)

    def step(t, carry):
        @pl.when(jnp.logical_and(t % SUBS == 0, t < NCHUNK))
        def _():
            whiten(t // SUBS)

        p = t - LAG * r

        @pl.when(jnp.logical_and(p >= 0, p < NCHUNK))
        def _():
            @pl.when(has_p)
            def _():
                forward(p).wait_recv()

            @pl.when(r < n - 1)
            def _():
                @pl.when(has_p)
                def _():
                    send_p[p] = (own[p] + recv_p[p].astype(F32)).astype(BF16)

                @pl.when(jnp.logical_not(has_p))
                def _():
                    send_p[p] = own[p].astype(BF16)

                forward(p).start()

        s = t - LAG * rr

        @pl.when(jnp.logical_and(s >= 0, s < NCHUNK))
        def _():
            @pl.when(has_s)
            def _():
                backward(s).wait_recv()

            @pl.when(give_s)
            def _():
                @pl.when(has_s)
                def _():
                    send_s[s] = (own[s] + recv_s[s].astype(F32)).astype(BF16)

                @pl.when(jnp.logical_not(has_s))
                def _():
                    send_s[s] = own[s].astype(BF16)

                backward(s).start()

        @pl.when(jnp.logical_and(t % SUBS == 1, t < pe_steps * SUBS))
        def _():
            i = t // SUBS
            codes = k_v[:, pl.ds(pl.multiple_of(i * WORDS, WORDS), WORDS)]
            second = lax.shift_right_logical(codes * 43, 8)
            first = codes - 6 * second
            table = jnp.full(codes.shape, 0xCA6953, jnp.int32)
            low = lax.shift_right_logical(table, 4 * first) & 15
            high = lax.shift_right_logical(table, 4 * second) & 15
            packed = (low + 16 * high).astype(F32).astype(BF16)
            spread = jnp.dot(packed, expand[...], preferred_element_type=F32).astype(jnp.int32)
            bit = jnp.left_shift(1, lax.broadcasted_iota(jnp.int32, spread.shape, 1) & 7)
            at = pl.ds(pl.multiple_of(i * 8 * WORDS, 8 * WORDS), 8 * WORDS)
            wv = w_v[:, at].astype(F32)
            uv = u_v[:, at].astype(F32)
            pe_ref[:, at] = (wv - jnp.where((spread & bit) != 0, wv + uv, 0.0)).astype(BF16)

        m = t - LAG * jnp.maximum(r, rr)

        @pl.when(jnp.logical_and(m >= 0, m < NCHUNK))
        def _():
            @pl.when(has_p)
            def _():
                own[m] = own[m] + recv_p[m].astype(F32)

            @pl.when(has_s)
            def _():
                own[m] = own[m] + recv_s[m].astype(F32)

            @pl.when(m % SUBS == SUBS - 1)
            def _():
                i = m // SUBS
                whole = own[pl.ds(pl.multiple_of(i * SUBS, SUBS), SUBS)].reshape(big, rank).astype(BF16)
                part = jnp.dot(pe_ref[:, pl.ds(pl.multiple_of(i * big, big), big)], whole, preferred_element_type=F32)
                acc[...] += part.reshape(acc.shape)

        return carry

    lax.fori_loop(0, NCHUNK + LAG * (n - 1), step, 0)

    def drain(j, carry):
        @pl.when(r < n - 1)
        def _():
            forward(j).wait_send()

        @pl.when(give_s)
        def _():
            backward(j).wait_send()

        return carry

    def peers(size, me):
        return [lax.rem(me + d, size) for d in range(1, size)]

    def swap(copies_out, copies_in):
        for one in copies_out:
            one.start()
        for one in copies_in:
            one.wait_recv()

    def exchange(src_of, dst, send, recv, axis, size, me):
        out = [copy_to(src_of(p), dst.at[me], send.at[p], recv.at[me], axis, p) for p in peers(size, me)]
        back = [copy_to(src_of(p), dst.at[p], send.at[p], recv.at[p], axis, p) for p in peers(size, me)]
        swap(out, back)
        return out

    sent = exchange(lambda p: acc.at[p], rs_recv, a_send, a_recv, "cols", nc, c)
    total = acc[c]
    for p in peers(nc, c):
        total = total + rs_recv[p]
    samp[c] = total
    sent += exchange(lambda p: samp.at[c], samp, b_send, b_recv, "cols", nc, c)
    sample = samp[...].reshape(local_rows, rank)
    gpart[...] = lax.dot_general(
        sample, sample, (((0,), (0,)), ((), ())), precision=HI, preferred_element_type=F32
    ).reshape(gpart.shape)
    sent += exchange(lambda p: gpart.at[c], gz, c_send, c_recv, "rows", n, r)
    total = gpart[c]
    for p in peers(n, r):
        total = total + gz[p]
    gfull[c] = total
    sent += exchange(lambda p: gfull.at[c], gfull, d_send, d_recv, "cols", nc, c)
    share, cq = out_ref.shape[0], width // q_count
    gw = gq * cq
    nq = q_count - gq
    plain = (n - 1) * nq
    lo, hi = lax.rem(r + n - 1, n), lax.rem(r + 1, n)
    near = [
        copy_to(pe_ref.at[:, 0:gw], pe_l, n_send.at[0], n_recv.at[0], "rows", hi),
        copy_to(pe_ref.at[:, 0:gw], pe_r, n_send.at[1], n_recv.at[1], "rows", lo),
        copy_to(a_ref, a_l, n_send.at[2], n_recv.at[2], "rows", hi),
        copy_to(a_ref, a_r, n_send.at[3], n_recv.at[3], "rows", lo),
    ]

    def start_near(i):
        @pl.when(r < n - 1)
        def _():
            near[i].start()

        @pl.when(r > 0)
        def _():
            near[i + 1].start()

    start_near(0)
    m_ref[...] = gfull[...].reshape(rank, rank)
    chol_steps(m_ref, inv_ref, rank, 8)
    basis = lax.dot_general(sample, inv_ref[...], (((1,), (1,)), ((), ())), precision=HI, preferred_element_type=F32)
    a_ref[...] = (root * basis).astype(BF16)
    start_near(2)

    def times(a, pe, at):
        return lax.dot_general(a[...], pe[:, at], (((0,), (0,)), ((), ())), preferred_element_type=F32).reshape(n, share, cq)

    def column(q):
        return pl.ds(pl.multiple_of(q * cq, cq), cq)

    def fill(i, carry):
        at = column(q_count - 1 - i)
        own2[:, :, at] = times(a_ref, pe_ref, at)
        return carry

    lax.fori_loop(0, q_count, fill, 0)

    def q_forward(b):
        return copy_to(q_send_p.at[b], q_recv_p.at[b], qsp_sem.at[b], qrp_sem.at[b], "rows", hi)

    def q_backward(b):
        return copy_to(q_send_s.at[b], q_recv_s.at[b], qss_sem.at[b], qrs_sem.at[b], "rows", lo)

    def first_sends(e, carry):
        at = column(gq + e % nq)

        @pl.when(r == 0)
        def _():
            q_send_p[e] = own2[n - 1 - e // nq, :, at].astype(BF16)
            q_forward(e).start()

        @pl.when(rr == 0)
        def _():
            q_send_s[e] = own2[e // nq, :, at].astype(BF16)
            q_backward(e).start()

        return carry

    lax.fori_loop(0, plain, first_sends, 0)

    def pass_on(b, first, least, place, target, t, base, at, copy, recv, send):
        @pl.when(jnp.logical_and(place > first, place <= target))
        def _():
            copy(b).wait_recv()
            base[t, :, at] = base[t, :, at] + recv[b].astype(F32)

        @pl.when(jnp.logical_and(place >= least, place < target))
        def _():
            send[b] = base[t, :, at].astype(BF16)
            copy(b).start()

    def chain(count, per, q0, b0, first, least, base_p, base_s):
        def step2(tau, carry):
            e = tau - LAG * r

            @pl.when(jnp.logical_and(e >= 0, e < count))
            def _():
                target = n - 1 - e // per
                pass_on(b0 + e, first, least, r, target, target, base_p, column(q0 + e % per), q_forward, q_recv_p, q_send_p)

            f = tau - LAG * rr

            @pl.when(jnp.logical_and(f >= 0, f < count))
            def _():
                target = n - 1 - f // per
                pass_on(b0 + f, first, least, rr, target, n - 1 - target, base_s, column(q0 + f % per), q_backward, q_recv_s, q_send_s)

            return carry

        lax.fori_loop(0, count + LAG * (n - 1), step2, 0)

    @pl.when(r > 0)
    def _():
        near[0].wait_recv()
        near[2].wait_recv()
        for q in range(gq):
            own_l[:, :, q * cq:(q + 1) * cq] = times(a_l, pe_l, slice(q * cq, (q + 1) * cq))

    @pl.when(r < n - 1)
    def _():
        near[1].wait_recv()
        near[3].wait_recv()
        for q in range(gq):
            own_r[:, :, q * cq:(q + 1) * cq] = times(a_r, pe_r, slice(q * cq, (q + 1) * cq))

    chain((n - 1) * gq, gq, 0, plain, 1, 1, own_l, own_r)
    chain(plain, nq, gq, 0, 0, 1, own2, own2)

    @pl.when(r > 0)
    def _():
        own2[r, :, 0:gw] = own2[r, :, 0:gw] + own_l[r]

    @pl.when(r < n - 1)
    def _():
        own2[r, :, 0:gw] = own2[r, :, 0:gw] + own_r[r]

    out_ref[...] = (own2[r] * (1.0 / root)).astype(BF16)

    lax.fori_loop(0, NCHUNK, drain, 0)

    def drain_second(count, per, b0, first):
        def one_drain(e, carry):
            target = n - 1 - e // per

            @pl.when(jnp.logical_and(r >= first, r < target))
            def _():
                q_forward(b0 + e).wait_send()

            @pl.when(jnp.logical_and(rr >= first, rr < target))
            def _():
                q_backward(b0 + e).wait_send()

            return carry

        lax.fori_loop(0, count, one_drain, 0)

    drain_second(plain, nq, 0, 0)
    drain_second((n - 1) * gq, gq, plain, 1)

    @pl.when(r < n - 1)
    def _():
        near[0].wait_send()
        near[2].wait_send()

    @pl.when(r > 0)
    def _():
        near[1].wait_send()
        near[3].wait_send()

    for one in sent:
        one.wait_send()


def adapters(n, nc, root, weight, update, codes, factor, sketch):
    rows, width = weight.shape
    block, depth = factor.shape
    rank = sketch.shape[1]
    ck = block // NCHUNK
    chunks = (NCHUNK, ck, rank)
    q_count = max(2, 32 // n)
    gq = max(1, q_count * GATHER // 8)
    gw = gq * (width // q_count)
    items = ((n - 1) * q_count, rank // n, width // q_count)
    vm = pl.BlockSpec(memory_space=pltpu.VMEM)
    dma = pltpu.SemaphoreType.DMA
    return pl.pallas_call(
        functools.partial(whole_kernel, n, nc, q_count, gq, root),
        out_shape=(jax.ShapeDtypeStruct((rows, rank), BF16), jax.ShapeDtypeStruct((rank // n, width), BF16)),
        in_specs=[pl.BlockSpec(memory_space=pl.ANY)] * 5,
        out_specs=(vm, vm),
        scratch_shapes=[
            pltpu.VMEM((rows, width), BF16),
            pltpu.VMEM((rows, width), BF16),
            pltpu.VMEM((rows, width), BF16),
            pltpu.VMEM(codes.shape, jnp.int32),
            pltpu.VMEM(sketch.shape, BF16),
            pltpu.VMEM((2, SUBS * ck, depth), BF16),
            pltpu.VMEM((WORDS, 8 * WORDS), BF16),
            pltpu.VMEM(chunks, F32),
            pltpu.VMEM(chunks, BF16),
            pltpu.VMEM(chunks, BF16),
            pltpu.VMEM(chunks, BF16),
            pltpu.VMEM(chunks, BF16),
            pltpu.VMEM((nc, rows // nc, rank), F32),
            pltpu.VMEM((nc, rows // nc, rank), F32),
            pltpu.VMEM((nc, rows // nc, rank), F32),
            pltpu.VMEM((nc, rank // nc, rank), F32),
            pltpu.VMEM((n, rank // nc, rank), F32),
            pltpu.VMEM((nc, rank // nc, rank), F32),
            dma((4,)),
            dma((2,)),
            dma((NCHUNK,)),
            dma((NCHUNK,)),
            dma((NCHUNK,)),
            dma((NCHUNK,)),
            dma((nc,)),
            dma((nc,)),
            dma((nc,)),
            dma((nc,)),
            dma((n,)),
            dma((n,)),
            dma((nc,)),
            dma((nc,)),
            pltpu.VMEM((rank, rank), F32),
            pltpu.VMEM((rank, rank), F32),
            pltpu.VMEM((rows, rank), BF16),
            pltpu.VMEM((rows, rank), BF16),
            pltpu.VMEM((rows, gw), BF16),
            pltpu.VMEM((rows, gw), BF16),
            pltpu.VMEM((n, rank // n, width), F32),
            pltpu.VMEM((n, rank // n, gw), F32),
            pltpu.VMEM((n, rank // n, gw), F32),
        ]
        + [pltpu.VMEM(items, BF16)] * 4
        + [dma((items[0],))] * 4
        + [dma((4,))] * 2,
        compiler_params=pltpu.CompilerParams(collective_id=0, has_side_effects=True, vmem_limit_bytes=58 << 20),
        name="adapters",
    )(weight, update, codes, factor, sketch)


def shards(n, nc, weight, update, keep_codes, chol_factor, sketch):
    root = math.sqrt(weight.shape[0] * n)
    return adapters(n, nc, root, weight, update, keep_codes, chol_factor, sketch)


def solution(mesh):
    in_specs = (
        P(("layers", "rows"), "cols"),
        P(("layers", "rows"), "cols"),
        P(("layers", "rows"), "cols"),
        P(("layers", "cols"), "rows"),
        P("rows", None),
    )
    out_specs = (P(("layers", "rows"), None), P(("layers", "rows"), "cols"))
    body = functools.partial(shards, mesh.shape["rows"], mesh.shape["cols"])
    return jax.shard_map(body, mesh=mesh, in_specs=in_specs, out_specs=out_specs, check_vma=False)
```
